512 devices in a mesh: head: 4 (over y_lo, core), qctx: 16 (over z), kctx: 8 (over x, y_hi).
Axes of the slice: x: 4, y: 4 (y_hi: 2, y_lo: 2; y = y_hi * 2 + y_lo), z: 16, core: 2. Of those that a mesh axis runs over, the one named last changes fastest.
Arguments:
- queries: bfloat16 [24576, 8192], P(('qctx', 'kctx'), 'head'), may hold values from -40 to 40
- keys: bfloat16 [24576, 512], P(('qctx', 'kctx'), 'head'), may hold values from -40 to 40
- values: bfloat16 [24576, 512], P(('qctx', 'kctx'), 'head'), may hold values from -6 to 6
- doc_lengths: int32 [16], replicated, may hold values from 1 to 3072, 24576 in all
Outputs:
- attended: bfloat16 [24576, 8192], P(('qctx', 'kctx'), 'head')
The draws below stay inside these ranges and needn't reach their ends.
Inputs may be any that keep to these rules, and one draw needn't show every extreme that they name: `doc_lengths`: every document holds at most 3072 tokens and one holds exactly 3072; the lengths sum to 24576.
All inputs are finite; a program needn't handle non-finite values.
Results may differ from the reference program's by a relative error of at most 0.0049.
Values may be sent and summed in bfloat16 or wider, within the bound.
No kernel may reach another device: no remote copies, remote signals or barrier semaphores. Data moves between devices by JAX's collectives and lax.ppermute only.
A program may use at most 64 MiB of HBM per device.

```python
import math
import jax
import jax.numpy as jnp
import numpy as np
from jax import lax

HD = 128
QH = 64
KVH = 4
FINE = 192
REACH = 2
TOKENS = 24576
MAXDOC = 3072
NDOCS = 16
N_QCTX = 16
N_KCTX = 8


def shared_keys(key):
    normal_part = jnp.clip(jax.random.normal(jax.random.fold_in(key, 11), (TOKENS, KVH * HD), jnp.float32), -6.0, 6.0)
    return normal_part


def draw_keys(key, part):
    result = shared_keys(key)
    return result.astype(jnp.bfloat16)


def draw_queries(key, part):
    key = jax.random.fold_in(key, 5)
    result = jnp.clip(jax.random.normal(jax.random.fold_in(key, 1), (TOKENS, QH * HD), jnp.float32), -6.0, 6.0)
    return result.astype(jnp.bfloat16)


def block_scale(key, dims, cuts, low, top_value):
    gain, own = 1.0, jax.random.fold_in(key, 6)
    for dim, blocks in cuts:
        steps = jnp.exp(jax.random.uniform(jax.random.fold_in(own, dim), (blocks,), jnp.float32, low / len(cuts), top_value / len(cuts)))
        gain = gain * jnp.repeat(steps, dims[dim] // blocks).reshape([-1 if axis == dim else 1 for axis in range(len(dims))])
    return gain


def split_up(amount, total, limit, skew):
    portions = [(1 << 20) // math.isqrt(grade ** skew) + 1 for grade in range(2, amount + 1)]
    surplus, counts = total - limit - (amount - 1), [1] * (amount - 1)
    while surplus > 0:
        movable = [i for i in range(amount - 1) if counts[i] < limit]
        pool, remaining = sum([portions[i] for i in movable]), surplus
        for i in movable:
            addition = min(limit - counts[i], max(1, remaining * portions[i] // pool), surplus)
            counts[i] = counts[i] + addition
            surplus = surplus - addition
    return np.array([limit] + counts)


def ragged_sizes(stream_key, amount, total, most, lean):
    if amount == 2:
        one = jax.random.randint(stream_key, (), max(1, total - most), min(most, total - 1) + 1)
        return jnp.stack([one, total - one])
    tallies = jnp.asarray(split_up(amount, total, most, lean), jnp.int32)
    pairs = (amount - 1) // 2
    giver, receiver = tallies[1:1 + 2 * pairs:2], tallies[2:2 + 2 * pairs:2]
    slack = jnp.minimum(giver - 1, most - receiver)
    passed = jax.random.randint(jax.random.fold_in(stream_key, 1), (pairs,), 0, 1 << 20) % (slack + 1)
    tallies = tallies.at[1:1 + 2 * pairs:2].set(giver - passed).at[2:2 + 2 * pairs:2].set(receiver + passed)
    return tallies[jax.random.permutation(jax.random.fold_in(stream_key, 2), amount)]


def gaussian(own_key, shape, scale, limit, split=(), kind=jnp.bfloat16):
    drawn = scale * jax.random.normal(own_key, shape, jnp.float32)
    if split:
        drawn = drawn * block_scale(own_key, shape, split, -0.22, 0.18)
    return jnp.clip(drawn, -limit, limit).astype(kind)


def setup_inputs(seed: int = 0) -> dict:
    seeds = jax.random.split(jax.random.key(seed), 5)
    queries = draw_queries(jax.random.fold_in(seeds[4], 71), 0)
    keys = draw_keys(jax.random.fold_in(seeds[4], 71), 0)
    values = gaussian(seeds[2], (TOKENS, KVH * HD), 1.0, 6.0, ((0, 128), (1, 4)))
    doc_lengths = ragged_sizes(seeds[3], NDOCS, TOKENS, MAXDOC, 1).astype(jnp.int32)
    return dict(queries=queries, keys=keys, values=values, doc_lengths=doc_lengths)


def reference(queries, keys, values, doc_lengths):
    group_count = QH // KVH
    block_rows = FINE * N_KCTX
    window = (REACH + 1) * block_rows
    lead_rows = REACH * block_rows
    score_scale = HD ** -0.5
    starts = (jnp.cumsum(doc_lengths) - doc_lengths).astype(jnp.int32)
    positions = jnp.arange(TOKENS, dtype=jnp.int32)
    doc_first = jnp.max(jnp.where(starts[None, :] <= positions[:, None], starts[None, :], 0), axis=1).astype(jnp.int32)
    padded_keys = jnp.concatenate([jnp.zeros((lead_rows, KVH * HD), keys.dtype), keys], axis=0)
    padded_values = jnp.concatenate([jnp.zeros((lead_rows, KVH * HD), values.dtype), values], axis=0)

    def one_block(which_block):
        block_index = (which_block // KVH).astype(jnp.int32)
        head_index = (which_block % KVH).astype(jnp.int32)
        row_start = (block_index * block_rows).astype(jnp.int32)
        query_rows = lax.dynamic_slice(queries, (row_start, head_index * group_count * HD), (block_rows, group_count * HD))
        query_rows = query_rows.reshape(block_rows, group_count, HD).astype(jnp.float32)
        key_rows = lax.dynamic_slice(padded_keys, (row_start, head_index * HD), (window, HD)).astype(jnp.float32)
        value_rows = lax.dynamic_slice(padded_values, (row_start, head_index * HD), (window, HD)).astype(jnp.float32)
        query_pos = row_start + jnp.arange(block_rows, dtype=jnp.int32)
        key_pos = row_start - lead_rows + jnp.arange(window, dtype=jnp.int32)
        firsts = lax.dynamic_slice(doc_first, (row_start,), (block_rows,))
        scores = jnp.einsum("qgd,kd->gqk", query_rows, key_rows) * score_scale
        allowed = (key_pos[None, :] >= firsts[:, None]) & (key_pos[None, :] <= query_pos[:, None])
        top_score = jnp.max(jnp.where(allowed, scores, jnp.float32(-1e30)), axis=-1)
        weights = jnp.where(allowed, jnp.exp(scores - top_score[..., None]), jnp.float32(0.0))
        totals = jnp.sum(weights, axis=-1)
        rounded = lax.optimization_barrier(weights.astype(jnp.bfloat16))
        result = jnp.einsum("gqk,kd->gqd", rounded.astype(jnp.float32), value_rows) / totals[..., None]
        return result.astype(jnp.bfloat16)

    blocks = lax.map(one_block, jnp.arange(N_QCTX * KVH, dtype=jnp.int32))
    blocks = blocks.reshape(N_QCTX, KVH, group_count, block_rows, HD)
    return jnp.transpose(blocks, (0, 3, 1, 2, 4)).reshape(TOKENS, QH * HD)
```

```python
from functools import partial

import jax
import jax.numpy as jnp
from jax import lax
from jax.experimental import pallas as pl
from jax.experimental.pallas import tpu as pltpu
from jax.sharding import PartitionSpec as P

HD = 128
STEP = 4
SUB = 2
TILE = 512
SCALE = HD**-0.5 * 1.4426950408889634
SAFE = 100.0
FAR = -(2.0**100)

bf16 = jnp.bfloat16
f32 = jnp.float32


def product(a, b, dims):
    return lax.dot_general(a, b, (dims, ((), ())), preferred_element_type=f32)


def largest_norm(x):
    squares = (x.astype(f32) * x.astype(f32)).astype(bf16)
    sums = product(squares, jnp.ones((HD, HD), bf16), ((1,), (0,)))
    return jnp.max(sums) * 1.02


def kernel(first, last, *refs):
    if first:
        place, docs, q_ref, kv_ref, out_ref, plain_out, norm_out, kx, vx, qx, knorm = refs
    elif last:
        place, plain_in, norm_in, docs, q_ref, kv_ref, state_ref, out_ref, kx, vx, qx, knorm = refs
    else:
        place, plain_in, norm_in, docs, q_ref, kv_ref, state_ref, out_ref, plain_out, kx, vx, qx, knorm = refs
    step = pl.program_id(0)
    keys = kv_ref.shape[0]
    rows = q_ref.shape[0]
    tile = min(TILE, keys)
    starts, ends = docs[0:1, :], docs[1:2, :]

    @pl.when(step == 0)
    def _():
        kx[:, 0:HD] = kv_ref[:, 0:HD]
        vx[:, 0:HD] = kv_ref[:, HD:]
        at = lax.broadcasted_iota(jnp.int32, (keys, HD), 0)
        pos = place[1] + at - jnp.where(at >= place[2], place[3], 0)
        kx[:, HD:] = jnp.where((pos >= starts) & (pos < ends), 0.0, FAR).astype(bf16)
        vx[:, HD:] = jnp.ones((keys, HD), bf16)
        at = lax.broadcasted_iota(jnp.int32, (rows, HD), 0) + place[0]
        own = jnp.where((at >= starts) & (at < ends), 1.0, 0.0).astype(bf16)
        for h in range(STEP):
            qx[h * rows : (h + 1) * rows, HD:] = own
        knorm[0] = largest_norm(kv_ref[:, 0:HD])

    for h in range(STEP):
        qx[h * rows : (h + 1) * rows, 0:HD] = q_ref[:, h * HD : (h + 1) * HD]
    if first:
        qnorm = largest_norm(qx[:, 0:HD])
        norm_out[step] = qnorm
    else:
        qnorm = norm_in[step]
    plain = qnorm * knorm[0] <= (SAFE / SCALE) ** 2
    if not first:
        plain = plain & (plain_in[step] == 1)
    if not last:
        plain_out[step] = plain.astype(jnp.int32)

    def scores(q, k):
        s = product(q, k, ((1,), (1,))) * SCALE
        if first:
            heads = q.shape[0] // rows
            r = lax.broadcasted_iota(jnp.int32, (rows, keys), 0)
            c = lax.broadcasted_iota(jnp.int32, (rows, keys), 1)
            early = jnp.concatenate([c <= r] * heads, axis=0)
            s = jnp.where(early, s, FAR)
        return s

    def put(row, state):
        if last:
            for h in range(state.shape[0] // rows):
                part = state[h * rows : (h + 1) * rows]
                out = part[:, 0:HD] / jnp.broadcast_to(part[:, HD : HD + 1], (rows, HD))
                head = row // rows + h
                if isinstance(row, int):
                    out_ref[:, head * HD : (head + 1) * HD] = out.astype(bf16)
                else:
                    out_ref[:, pl.ds(pl.multiple_of(head * HD, HD), HD)] = out.astype(bf16)
        else:
            out_ref[pl.ds(row, state.shape[0]), :] = state

    @pl.when(plain)
    def _():
        size = SUB * rows
        for row in range(0, STEP * rows, size):
            state = None if first else state_ref[row : row + size, :]
            for key in range(0, keys, tile):
                s = scores(qx[row : row + size, :], kx[key : key + tile, :])
                update = product(jnp.exp2(s).astype(bf16), vx[key : key + tile, :], ((1,), (0,)))
                state = update if state is None else state + update
            if first:
                lane = lax.broadcasted_iota(jnp.int32, state.shape, 1)
                state = jnp.where(lane == 2 * HD - 1, 0.0, state)
            put(row, state)

    @pl.when(jnp.logical_not(plain))
    def _():
        def head(h, carry):
            row = pl.multiple_of(h * rows, rows)
            lane = lax.broadcasted_iota(jnp.int32, (rows, 2 * HD), 1)
            if first:
                state = jnp.where(lane == 2 * HD - 1, FAR, 0.0)
            else:
                state = state_ref[pl.ds(row, rows), :]
            for key in range(0, keys, tile):
                s = scores(qx[pl.ds(row, rows), :], kx[key : key + tile, :])
                old = state[:, 2 * HD - 1 :]
                top = jnp.maximum(old, jnp.max(s, axis=1, keepdims=True))
                weights = jnp.exp2(s - top).astype(bf16)
                update = product(weights, vx[key : key + tile, :], ((1,), (0,)))
                state = state * jnp.exp2(old - top) + update
                state = jnp.where(lane == 2 * HD - 1, top, state)
            put(row, state)
            return carry

        lax.fori_loop(0, STEP, head, 0)


def attend(first, last, place, docs, queries, kv, plain=None, norm=None, state=None):
    rows, width = queries.shape
    keys = kv.shape[0]
    heads = width // HD
    steps = heads // STEP
    smem = pl.BlockSpec(memory_space=pltpu.SMEM)
    whole = lambda shape: pl.BlockSpec(shape, lambda i: (0, 0))
    state_spec = pl.BlockSpec((STEP * rows, 2 * HD), lambda i: (i, 0))
    row_spec = pl.BlockSpec((rows, STEP * HD), lambda i: (0, i))
    in_specs = [smem] + ([] if first else [smem, smem])
    in_specs += [whole((2, HD)), row_spec, whole((keys, 2 * HD))] + ([] if first else [state_spec])
    args = [place] + ([] if first else [plain, norm]) + [docs, queries, kv] + ([] if first else [state])
    if last:
        out_shape = [jax.ShapeDtypeStruct(queries.shape, bf16)]
        out_specs = [row_spec]
    else:
        out_shape = [jax.ShapeDtypeStruct((heads * rows, 2 * HD), f32), jax.ShapeDtypeStruct((steps,), jnp.int32)]
        out_specs = [state_spec, smem]
    if first:
        out_shape.append(jax.ShapeDtypeStruct((steps,), f32))
        out_specs.append(smem)
    return pl.pallas_call(
        partial(kernel, first, last),
        out_shape=out_shape,
        grid=(steps,),
        in_specs=in_specs,
        out_specs=out_specs,
        scratch_shapes=[
            pltpu.VMEM((keys, 2 * HD), bf16),
            pltpu.VMEM((keys, 2 * HD), bf16),
            pltpu.VMEM((STEP * rows, 2 * HD), bf16),
            pltpu.SMEM((1,), f32),
        ],
        compiler_params=pltpu.CompilerParams(vmem_limit_bytes=40 * 2**20),
        cost_estimate=pl.CostEstimate(
            flops=8 * heads * rows * keys * HD,
            bytes_accessed=2 * rows * width + heads * rows * HD * 8,
            transcendentals=heads * rows * keys,
        ),
    )(*args)


def passed_along(x, by):
    count = lax.axis_size("qctx")
    return lax.ppermute(x, "qctx", [(i, i + by) for i in range(count - by)])


def shards(queries, keys, values, doc_lengths):
    rows = queries.shape[0]
    fine = lax.axis_size("kctx")
    block, part = lax.axis_index("qctx"), lax.axis_index("kctx")
    block_rows = fine * rows
    ends = jnp.cumsum(doc_lengths)
    docs = jnp.pad(jnp.stack([ends - doc_lengths, ends]), ((0, 0), (0, HD - ends.shape[0])))
    own_start = block * block_rows + part * rows

    def place(key_start, wrap_at):
        return jnp.stack([own_start, key_start, wrap_at, jnp.int32(block_rows)]).astype(jnp.int32)

    own = jnp.concatenate([keys, values], axis=1)
    one_back = passed_along(own, 1)
    two_back = passed_along(own, 2)
    later = jnp.arange(fine)[:, None, None] > part
    near = lax.all_to_all(jnp.where(later, own[None], one_back[None]), "kctx", 0, 0)
    far = lax.all_to_all(jnp.where(later, one_back[None], two_back[None]), "kctx", 0, 0)
    near, far = near.reshape(block_rows, 2 * HD), far.reshape(block_rows, 2 * HD)

    state, plain, norm = attend(True, False, place(own_start, rows), docs, queries, own)
    start = block * block_rows
    state, plain = attend(False, False, place(start, part * rows), docs, queries, near, plain, norm, state)
    return attend(False, True, place(start - block_rows, part * rows), docs, queries, far, plain, norm, state)[0]


def solution(mesh):
    placed = P(("qctx", "kctx"), "head")
    return jax.shard_map(
        shards, mesh=mesh, in_specs=(placed, placed, placed, P()), out_specs=placed, check_vma=False
    )
```

```python
from functools import partial

import jax
import jax.numpy as jnp
from jax import lax
from jax.experimental import pallas as pl
from jax.experimental.pallas import tpu as pltpu
from jax.sharding import PartitionSpec as P

HD = 128
SUB = 2
LEAN_TILE = 512
VMEM_BYTES = 50 * 2**20
PARTS = 2
TILE = 512
SCALE = HD**-0.5 * 1.4426950408889634
SAFE = 100.0
FAR = -(2.0**100)

bf16 = jnp.bfloat16
f32 = jnp.float32


def product(a, b, dims):
    return lax.dot_general(a, b, (dims, ((), ())), preferred_element_type=f32)


def largest_norm(x):
    squares = (x.astype(f32) * x.astype(f32)).astype(bf16)
    sums = product(squares, jnp.ones((HD, HD), bf16), ((1,), (0,)))
    return jnp.max(sums) * 1.02


def kernel(first, back, *refs):
    if first:
        lengths, q_ref, kv_ref, own_ref, out_hbm, guard_out, *scratch = refs
    else:
        lengths, guard_in, q_ref, kv_ref, state_hbm, out_hbm, *scratch = refs
    state_ref, out_ref, kx, vx, sems = scratch
    keys = kv_ref.shape[0]
    rows, width = q_ref.shape
    heads = width // HD
    size = SUB * rows
    every = keys + rows if first else keys
    block, part = lax.axis_index("qctx"), lax.axis_index("kctx")

    def copy_out(i):
        if first:
            here = pl.ds(i * (heads // PARTS) * rows, heads // PARTS * rows)
            return pltpu.make_async_copy(state_ref.at[here], out_hbm.at[here], sems.at[i])
        here = pl.ds(i * (width // PARTS), width // PARTS)
        return pltpu.make_async_copy(out_ref.at[:, here], out_hbm.at[:, here], sems.at[i])

    if not first:
        get_state = pltpu.make_async_copy(state_hbm, state_ref, sems.at[PARTS])
        get_state.start()

    lane = lax.broadcasted_iota(jnp.int32, (1, HD), 1)
    starts = jnp.zeros((1, HD), jnp.int32)
    ends = jnp.zeros((1, HD), jnp.int32)
    run = jnp.int32(0)
    for d in range(lengths.shape[0]):
        starts = jnp.where(lane == d, run, starts)
        run = run + lengths[d]
        ends = jnp.where(lane == d, run, ends)
    at = lax.broadcasted_iota(jnp.int32, (keys, HD), 0)
    pos = block * keys + at - jnp.where(at >= part * rows, keys, 0) - back * keys
    kx[0:keys, HD:] = jnp.where((pos >= starts) & (pos < ends), 0.0, FAR).astype(bf16)
    at = lax.broadcasted_iota(jnp.int32, (rows, HD), 0) + block * keys + part * rows
    mine = (at >= starts) & (at < ends)
    onehot = jnp.where(mine, 1.0, 0.0).astype(bf16)
    vx[:, HD:] = jnp.ones((every, HD), bf16)
    kx[0:keys, 0:HD] = kv_ref[:, 0:HD]
    vx[0:keys, 0:HD] = kv_ref[:, HD:]
    knorm = largest_norm(kv_ref[:, 0:HD])
    if first:
        kx[keys:, HD:] = jnp.where(mine, 0.0, FAR).astype(bf16)
        kx[keys:, 0:HD] = own_ref[:, 0:HD]
        vx[keys:, 0:HD] = own_ref[:, HD:]
        knorm = jnp.maximum(knorm, largest_norm(own_ref[:, 0:HD]))
        qnorm = largest_norm(q_ref[:, 0:HD])
        for h in range(1, heads):
            qnorm = jnp.maximum(qnorm, largest_norm(q_ref[:, h * HD : (h + 1) * HD]))
    else:
        qnorm = guard_in[1]
    plain = qnorm * knorm <= (SAFE / SCALE) ** 2
    if first:
        guard_out[0] = plain.astype(f32)
        guard_out[1] = qnorm
    else:
        plain = plain & (guard_in[0] == 1.0)
        get_state.wait()

    def scores(q, key, count):
        s = product(q, kx[key : key + count, :], ((1,), (1,))) * SCALE
        if key == keys:
            r = lax.broadcasted_iota(jnp.int32, (rows, rows), 0)
            c = lax.broadcasted_iota(jnp.int32, (rows, rows), 1)
            s = jnp.where(jnp.concatenate([c <= r] * (q.shape[0] // rows), axis=0), s, FAR)
        return s

    def tiles(tile):
        return [(key, tile) for key in range(0, keys, tile)] + ([(keys, rows)] if first else [])

    def divided(part):
        total = jnp.broadcast_to(part[:, HD : HD + 1], (rows, HD))
        return (part[:, 0:HD] / total).astype(bf16)

    @pl.when(plain)
    def _():
        for i in range(PARTS):
            for head in range(i * heads // PARTS, (i + 1) * heads // PARTS, SUB):
                here = slice(head * rows, head * rows + size)
                group = range(head, head + SUB)
                q = [jnp.concatenate([q_ref[:, h * HD : (h + 1) * HD], onehot], axis=1) for h in group]
                q = jnp.concatenate(q, axis=0)
                state = None if first else state_ref[here, :]
                for key, count in tiles(TILE):
                    weights = jnp.exp2(scores(q, key, count)).astype(bf16)
                    update = product(weights, vx[key : key + count, :], ((1,), (0,)))
                    state = update if state is None else state + update
                if first:
                    lanes = lax.broadcasted_iota(jnp.int32, state.shape, 1)
                    state_ref[here, :] = jnp.where(lanes == 2 * HD - 1, 0.0, state)
                else:
                    for n, h in enumerate(group):
                        out_ref[:, h * HD : (h + 1) * HD] = divided(state[n * rows : (n + 1) * rows])
            copy_out(i).start()

    @pl.when(jnp.logical_not(plain))
    def _():
        def one(head, carry):
            row = pl.multiple_of(head * rows, rows)
            column = pl.multiple_of(head * HD, HD)
            lanes = lax.broadcasted_iota(jnp.int32, (rows, 2 * HD), 1)
            if first:
                state = jnp.where(lanes == 2 * HD - 1, FAR, 0.0)
            else:
                state = state_ref[pl.ds(row, rows), :]
            q = jnp.concatenate([q_ref[:, pl.ds(column, HD)], onehot], axis=1)
            for key, count in reversed(tiles(LEAN_TILE)):
                s = scores(q, key, count)
                old = state[:, 2 * HD - 1 :]
                top = jnp.maximum(old, jnp.max(s, axis=1, keepdims=True))
                weights = jnp.exp2(s - top).astype(bf16)
                update = product(weights, vx[key : key + count, :], ((1,), (0,)))
                state = state * jnp.exp2(old - top) + update
                state = jnp.where(lanes == 2 * HD - 1, top, state)
            if first:
                state_ref[pl.ds(row, rows), :] = state
            else:
                out_ref[:, pl.ds(column, HD)] = divided(state)
            return carry

        lax.fori_loop(0, heads, one, 0)
        for i in range(PARTS):
            copy_out(i).start()

    for i in range(PARTS):
        copy_out(i).wait()


def attend(first, back, doc_lengths, queries, kv, *rest):
    rows, width = queries.shape
    keys = kv.shape[0]
    every = keys + rows if first else keys
    heads = width // HD
    smem = pl.BlockSpec(memory_space=pltpu.SMEM)
    vmem = pl.BlockSpec(memory_space=pltpu.VMEM)
    hbm = pl.BlockSpec(memory_space=pltpu.HBM)
    if first:
        args = (doc_lengths, queries, kv) + rest
        in_specs = [smem, vmem, vmem, vmem]
        out_shape = [jax.ShapeDtypeStruct((heads * rows, 2 * HD), f32), jax.ShapeDtypeStruct((2,), f32)]
        out_specs = [hbm, smem]
    else:
        state, guard = rest
        args = (doc_lengths, guard, queries, kv, state)
        in_specs = [smem, smem, vmem, vmem, hbm]
        out_shape = jax.ShapeDtypeStruct(queries.shape, bf16)
        out_specs = hbm
    return pl.pallas_call(
        partial(kernel, first, back),
        out_shape=out_shape,
        in_specs=in_specs,
        out_specs=out_specs,
        scratch_shapes=[
            pltpu.VMEM((heads * rows, 2 * HD), f32),
            pltpu.VMEM((8, HD) if first else (rows, width), bf16),
            pltpu.VMEM((every, 2 * HD), bf16),
            pltpu.VMEM((every, 2 * HD), bf16),
            pltpu.SemaphoreType.DMA((PARTS + 1,)),
        ],
        compiler_params=pltpu.CompilerParams(vmem_limit_bytes=VMEM_BYTES),
        cost_estimate=pl.CostEstimate(
            flops=8 * heads * rows * every * HD,
            bytes_accessed=2 * rows * width + heads * rows * HD * 8,
            transcendentals=heads * rows * every,
        ),
    )(*args)


def passed_along(x, by):
    count = lax.axis_size("qctx")
    return lax.ppermute(x, "qctx", [(i, i + by) for i in range(count - by)])


def to_parts(upward, downward):
    fine = lax.axis_size("kctx")
    later = jnp.arange(fine)[:, None, None] > lax.axis_index("kctx")
    return jnp.where(later, upward[None], downward[None])


def beside(keys, values):
    low = jnp.array(-jnp.inf, bf16)
    keys = lax.pad(keys, low, ((0, 0, 0), (0, HD, 0)))
    return jnp.maximum(keys, lax.pad(values, low, ((0, 0, 0), (HD, 0, 0))))


def shards(queries, keys, values, doc_lengths):
    block_rows = lax.axis_size("kctx") * queries.shape[0]
    own = beside(keys, values)
    one_back = passed_along(own, 1)
    near_parts, held = lax.optimization_barrier((to_parts(own, one_back), one_back))
    near = lax.all_to_all(near_parts, "kctx", 0, 0).reshape(block_rows, 2 * HD)
    two_back = passed_along(held, 1)
    far = lax.all_to_all(to_parts(held, two_back), "kctx", 0, 0).reshape(block_rows, 2 * HD)
    carried = attend(True, 0, doc_lengths, queries, near, own)
    return attend(False, 1, doc_lengths, queries, far, *carried)


def solution(mesh):
    placed = P(("qctx", "kctx"), "head")
    return jax.shard_map(
        shards, mesh=mesh, in_specs=(placed, placed, placed, P()), out_specs=placed, check_vma=False
    )
```

```python
from functools import partial

import jax
import jax.numpy as jnp
from jax import lax
from jax.experimental import pallas as pl
from jax.experimental.pallas import tpu as pltpu
from jax.sharding import PartitionSpec as P

HD = 128
SUB = 2
LEAN_TILE = 512
VMEM_BYTES = 50 * 2**20
PARTS = 2
TILE = 512
SCALE = HD**-0.5 * 1.4426950408889634
SAFE = 100.0
FAR = -(2.0**100)

bf16 = jnp.bfloat16
f32 = jnp.float32


def product(a, b, dims):
    return lax.dot_general(a, b, (dims, ((), ())), preferred_element_type=f32)


def largest_norm(x):
    squares = (x.astype(f32) * x.astype(f32)).astype(bf16)
    sums = product(squares, jnp.ones((HD, HD), bf16), ((1,), (0,)))
    return jnp.max(sums) * 1.02


def kernel(first, back, *refs):
    if first:
        lengths, q_ref, kv_ref, own_ref, out_hbm, guard_out, *scratch = refs
    else:
        lengths, guard_in, q_ref, kv_ref, state_hbm, out_hbm, *scratch = refs
    state_ref, out_ref, kx, vx, sems = scratch
    keys = kv_ref.shape[0]
    rows, width = q_ref.shape
    heads = width // HD
    size = SUB * rows
    every = keys + rows if first else keys
    block, part = lax.axis_index("qctx"), lax.axis_index("kctx")

    def copy_out(i):
        if first:
            here = pl.ds(i * (heads // PARTS) * rows, heads // PARTS * rows)
            return pltpu.make_async_copy(state_ref.at[here], out_hbm.at[here], sems.at[i])
        here = pl.ds(i * (width // PARTS), width // PARTS)
        return pltpu.make_async_copy(out_ref.at[:, here], out_hbm.at[:, here], sems.at[i])

    if not first:
        get_state = pltpu.make_async_copy(state_hbm, state_ref, sems.at[PARTS])
        get_state.start()

    lane = lax.broadcasted_iota(jnp.int32, (1, HD), 1)
    starts = jnp.zeros((1, HD), jnp.int32)
    ends = jnp.zeros((1, HD), jnp.int32)
    run = jnp.int32(0)
    for d in range(lengths.shape[0]):
        starts = jnp.where(lane == d, run, starts)
        run = run + lengths[d]
        ends = jnp.where(lane == d, run, ends)
    at = lax.broadcasted_iota(jnp.int32, (keys, HD), 0)
    pos = block * keys + at - jnp.where(at >= part * rows, keys, 0) - back * keys
    kx[0:keys, HD:] = jnp.where((pos >= starts) & (pos < ends), 0.0, FAR).astype(bf16)
    at = lax.broadcasted_iota(jnp.int32, (rows, HD), 0) + block * keys + part * rows
    mine = (at >= starts) & (at < ends)
    onehot = jnp.where(mine, 1.0, 0.0).astype(bf16)
    vx[:, HD:] = jnp.ones((every, HD), bf16)
    kx[0:keys, 0:HD] = kv_ref[:, 0:HD]
    vx[0:keys, 0:HD] = kv_ref[:, HD:]
    if not first:
        get_state.wait()
    knorm = largest_norm(kv_ref[:, 0:HD])
    if first:
        kx[keys:, HD:] = jnp.where(mine, 0.0, FAR).astype(bf16)
        kx[keys:, 0:HD] = own_ref[:, 0:HD]
        vx[keys:, 0:HD] = own_ref[:, HD:]
        knorm = jnp.maximum(knorm, largest_norm(own_ref[:, 0:HD]))
        qnorm = largest_norm(q_ref[:, 0:HD])
        for h in range(1, heads):
            qnorm = jnp.maximum(qnorm, largest_norm(q_ref[:, h * HD : (h + 1) * HD]))
    else:
        qnorm = guard_in[1]
    plain = qnorm * knorm <= (SAFE / SCALE) ** 2
    if first:
        guard_out[0] = plain.astype(f32)
        guard_out[1] = qnorm
    else:
        plain = plain & (guard_in[0] == 1.0)

    def scores(q, key, count):
        s = product(q, kx[key : key + count, :], ((1,), (1,))) * SCALE
        if key == keys:
            r = lax.broadcasted_iota(jnp.int32, (rows, rows), 0)
            c = lax.broadcasted_iota(jnp.int32, (rows, rows), 1)
            s = jnp.where(jnp.concatenate([c <= r] * (q.shape[0] // rows), axis=0), s, FAR)
        return s

    def tiles(tile):
        return [(key, tile) for key in range(0, keys, tile)] + ([(keys, rows)] if first else [])

    def divided(part):
        total = jnp.broadcast_to(part[:, HD : HD + 1], (rows, HD))
        return (part[:, 0:HD] / total).astype(bf16)

    for i in range(PARTS):
        for head in range(i * heads // PARTS, (i + 1) * heads // PARTS, SUB):
            here = slice(head * rows, head * rows + size)
            group = range(head, head + SUB)
            q = [jnp.concatenate([q_ref[:, h * HD : (h + 1) * HD], onehot], axis=1) for h in group]
            q = jnp.concatenate(q, axis=0)
            state = None if first else state_ref[here, :]
            for key, count in tiles(TILE):
                weights = jnp.exp2(scores(q, key, count)).astype(bf16)
                update = product(weights, vx[key : key + count, :], ((1,), (0,)))
                state = update if state is None else state + update
            if first:
                lanes = lax.broadcasted_iota(jnp.int32, state.shape, 1)
                state_ref[here, :] = jnp.where(lanes == 2 * HD - 1, 0.0, state)
            else:
                for n, h in enumerate(group):
                    out_ref[:, h * HD : (h + 1) * HD] = divided(state[n * rows : (n + 1) * rows])
        copy_out(i).start()
    for i in range(PARTS):
        copy_out(i).wait()

    @pl.when(jnp.logical_not(plain))
    def _():
        def one(head, carry):
            row = pl.multiple_of(head * rows, rows)
            column = pl.multiple_of(head * HD, HD)
            lanes = lax.broadcasted_iota(jnp.int32, (rows, 2 * HD), 1)
            if first:
                state = jnp.where(lanes == 2 * HD - 1, FAR, 0.0)
            else:
                state = state_ref[pl.ds(row, rows), :]
            q = jnp.concatenate([q_ref[:, pl.ds(column, HD)], onehot], axis=1)
            for key, count in reversed(tiles(LEAN_TILE)):
                s = scores(q, key, count)
                old = state[:, 2 * HD - 1 :]
                top = jnp.maximum(old, jnp.max(s, axis=1, keepdims=True))
                weights = jnp.exp2(s - top).astype(bf16)
                update = product(weights, vx[key : key + count, :], ((1,), (0,)))
                state = state * jnp.exp2(old - top) + update
                state = jnp.where(lanes == 2 * HD - 1, top, state)
            if first:
                state_ref[pl.ds(row, rows), :] = state
            else:
                out_ref[:, pl.ds(column, HD)] = divided(state)
            return carry

        lax.fori_loop(0, heads, one, 0)
        for i in range(PARTS):
            copy_out(i).start()
        for i in range(PARTS):
            copy_out(i).wait()


def attend(first, back, doc_lengths, queries, kv, *rest):
    rows, width = queries.shape
    keys = kv.shape[0]
    every = keys + rows if first else keys
    heads = width // HD
    smem = pl.BlockSpec(memory_space=pltpu.SMEM)
    vmem = pl.BlockSpec(memory_space=pltpu.VMEM)
    hbm = pl.BlockSpec(memory_space=pltpu.HBM)
    if first:
        args = (doc_lengths, queries, kv) + rest
        in_specs = [smem, vmem, vmem, vmem]
        out_shape = [jax.ShapeDtypeStruct((heads * rows, 2 * HD), f32), jax.ShapeDtypeStruct((2,), f32)]
        out_specs = [hbm, smem]
    else:
        state, guard = rest
        args = (doc_lengths, guard, queries, kv, state)
        in_specs = [smem, smem, vmem, vmem, hbm]
        out_shape = jax.ShapeDtypeStruct(queries.shape, bf16)
        out_specs = hbm
    return pl.pallas_call(
        partial(kernel, first, back),
        out_shape=out_shape,
        in_specs=in_specs,
        out_specs=out_specs,
        scratch_shapes=[
            pltpu.VMEM((heads * rows, 2 * HD), f32),
            pltpu.VMEM((8, HD) if first else (rows, width), bf16),
            pltpu.VMEM((every, 2 * HD), bf16),
            pltpu.VMEM((every, 2 * HD), bf16),
            pltpu.SemaphoreType.DMA((PARTS + 1,)),
        ],
        compiler_params=pltpu.CompilerParams(vmem_limit_bytes=VMEM_BYTES),
        cost_estimate=pl.CostEstimate(
            flops=8 * heads * rows * every * HD,
            bytes_accessed=2 * rows * width + heads * rows * HD * 8,
            transcendentals=heads * rows * every,
        ),
    )(*args)


def passed_along(x, by):
    count = lax.axis_size("qctx")
    return lax.ppermute(x, "qctx", [(i, i + by) for i in range(count - by)])


def to_parts(upward, downward):
    fine = lax.axis_size("kctx")
    later = jnp.arange(fine)[:, None, None] > lax.axis_index("kctx")
    return jnp.where(later, upward[None], downward[None])


def beside(keys, values):
    low = jnp.array(-jnp.inf, bf16)
    keys = lax.pad(keys, low, ((0, 0, 0), (0, HD, 0)))
    return jnp.maximum(keys, lax.pad(values, low, ((0, 0, 0), (HD, 0, 0))))


def shards(queries, keys, values, doc_lengths):
    block_rows = lax.axis_size("kctx") * queries.shape[0]
    own = beside(keys, values)
    one_back = passed_along(own, 1)
    near_parts, held = lax.optimization_barrier((to_parts(own, one_back), one_back))
    near = lax.all_to_all(near_parts, "kctx", 0, 0).reshape(block_rows, 2 * HD)
    two_back = passed_along(held, 1)
    far = lax.all_to_all(to_parts(held, two_back), "kctx", 0, 0).reshape(block_rows, 2 * HD)
    carried = attend(True, 0, doc_lengths, queries, near, own)
    return attend(False, 1, doc_lengths, queries, far, *carried)


def solution(mesh):
    placed = P(("qctx", "kctx"), "head")
    return jax.shard_map(
        shards, mesh=mesh, in_specs=(placed, placed, placed, P()), out_specs=placed, check_vma=False
    )
```

```python
from functools import partial

import jax
import jax.numpy as jnp
from jax import lax
from jax.experimental import pallas as pl
from jax.experimental.pallas import tpu as pltpu
from jax.sharding import PartitionSpec as P

HD = 128
SUB = 2
VMEM_BYTES = (52 * 2**20, 50 * 2**20, 50 * 2**20)
PARTS = 2
CUT = 128
TILE = 512
SCALE = HD**-0.5 * 1.4426950408889634
SAFE = 100.0
FAR = -(2.0**100)

bf16 = jnp.bfloat16
f32 = jnp.float32


def product(a, b, dims):
    return lax.dot_general(a, b, (dims, ((), ())), preferred_element_type=f32)


def largest_norm(x):
    squares = (x.astype(f32) * x.astype(f32)).astype(bf16)
    sums = product(squares, jnp.ones((HD, HD), bf16), ((1,), (0,)))
    return jnp.max(sums) * 1.02


def kernel(stage, back, ring, *refs):
    lengths, *refs = refs
    if stage:
        guard_in, *refs = refs
    q_ref, *refs = refs
    kv_refs, refs = refs[: len(back) or 1], refs[len(back) or 1 :]
    states, refs = (refs[:2], refs[2:]) if stage == 2 else ([], refs)
    out_hbm, *refs = refs
    if stage < 2:
        guard_out, *refs = refs
    state_ref, held_ref, out_ref, kx, vx, sems = refs
    keys = kx.shape[0]
    rows, width = q_ref.shape
    heads = width // HD
    size = SUB * rows
    block, part = lax.axis_index("qctx"), lax.axis_index("kctx")

    def copy_out(i):
        if stage < 2:
            here = pl.ds(i * (heads // PARTS) * rows, heads // PARTS * rows)
            return pltpu.make_async_copy(state_ref.at[0, here], out_hbm.at[here], sems.at[i])
        here = pl.ds(i * (width // PARTS), width // PARTS)
        return pltpu.make_async_copy(out_ref.at[:, here], out_hbm.at[:, here], sems.at[i])

    get_states = [
        pltpu.make_async_copy(state, state_ref.at[n], sems.at[PARTS + n]) for n, state in enumerate(states)
    ]
    for get in get_states:
        get.start()

    lane = lax.broadcasted_iota(jnp.int32, (1, HD), 1)
    starts = jnp.zeros((1, HD), jnp.int32)
    ends = jnp.zeros((1, HD), jnp.int32)
    run = jnp.int32(0)
    for d in range(lengths.shape[0]):
        starts = jnp.where(lane == d, run, starts)
        run = run + lengths[d]
        ends = jnp.where(lane == d, run, ends)
    at = lax.broadcasted_iota(jnp.int32, (rows, HD), 0) + block * ring + part * rows
    mine = (at >= starts) & (at < ends)
    onehot = jnp.where(mine, 1.0, 0.0).astype(bf16)
    if stage == 0:
        kx[:, HD:] = jnp.where(mine, 0.0, FAR).astype(bf16)
    row = 0
    for kv_ref, (slabs, offset) in zip(kv_refs, back):
        slots = ring // rows
        count = kv_ref.shape[0] // slots
        for j in range(slots):
            base = (block - slabs) * ring + j * rows + offset - jnp.where(j >= part, ring, 0)
            pos = lax.broadcasted_iota(jnp.int32, (count, HD), 0) + base
            apart = jnp.where((pos >= starts) & (pos < ends), 0.0, FAR)
            kx[row + j * count : row + (j + 1) * count, HD:] = apart.astype(bf16)
        row += kv_ref.shape[0]
    row = 0
    knorm = f32(0.0)
    for kv_ref in kv_refs:
        here = slice(row, row + kv_ref.shape[0])
        kx[here, 0:HD] = kv_ref[:, 0:HD]
        vx[here, 0:HD] = kv_ref[:, HD:]
        knorm = jnp.maximum(knorm, largest_norm(kv_ref[:, 0:HD]))
        row += kv_ref.shape[0]
    vx[:, HD:] = jnp.ones((keys, HD), bf16)
    if stage == 0:
        qnorm = largest_norm(q_ref[:, 0:HD])
        for h in range(1, heads):
            qnorm = jnp.maximum(qnorm, largest_norm(q_ref[:, h * HD : (h + 1) * HD]))
    else:
        qnorm = guard_in[1]
    plain = qnorm * knorm <= (SAFE / SCALE) ** 2
    if stage:
        plain = plain & (guard_in[0] == 1.0)
    if stage < 2:
        guard_out[0] = plain.astype(f32)
        guard_out[1] = qnorm

    def scores(q, key, count):
        s = product(q, kx[key : key + count, :], ((1,), (1,))) * SCALE
        if stage == 0:
            r = lax.broadcasted_iota(jnp.int32, (rows, count), 0)
            c = lax.broadcasted_iota(jnp.int32, (rows, count), 1) + key
            s = jnp.where(jnp.concatenate([c <= r] * (q.shape[0] // rows), axis=0), s, FAR)
        return s

    tiles = [(key, min(TILE, keys - key)) for key in range(0, keys, TILE)]

    def divided(part):
        total = jnp.broadcast_to(part[:, HD : HD + 1], (rows, HD))
        return (part[:, 0:HD] / total).astype(bf16)

    def update_of(head):
        q = [jnp.concatenate([q_ref[:, h * HD : (h + 1) * HD], onehot], axis=1) for h in range(head, head + SUB)]
        q = jnp.concatenate(q, axis=0)
        total = None
        for key, count in tiles:
            weights = jnp.exp2(scores(q, key, count)).astype(bf16)
            update = product(weights, vx[key : key + count, :], ((1,), (0,)))
            total = update if total is None else total + update
        return total

    def finish(head, update):
        here = slice(head * rows, head * rows + size)
        state = state_ref[0, here, :] + state_ref[1, here, :] + update
        for n in range(SUB):
            column = (head + n) * HD
            out_ref[:, column : column + HD] = divided(state[n * rows : (n + 1) * rows])

    for i in range(PARTS):
        group = range(i * heads // PARTS, (i + 1) * heads // PARTS, SUB)
        for head in group:
            here = slice(head * rows, head * rows + size)
            if stage < 2:
                update = update_of(head)
                lanes = lax.broadcasted_iota(jnp.int32, update.shape, 1)
                state_ref[0, here, :] = jnp.where(lanes == 2 * HD - 1, 0.0, update)
            elif i == 0:
                held_ref[here, :] = update_of(head)
            else:
                finish(head, update_of(head))
        if stage == 2 and i == 0:
            for get in get_states:
                get.wait()
            for head in group:
                finish(head, held_ref[head * rows : head * rows + size, :])
        copy_out(i).start()
    for i in range(PARTS):
        copy_out(i).wait()

    @pl.when(jnp.logical_not(plain))
    def _():
        def one(head, carry):
            row = pl.multiple_of(head * rows, rows)
            column = pl.multiple_of(head * HD, HD)
            lanes = lax.broadcasted_iota(jnp.int32, (rows, 2 * HD), 1)
            last_lane = lanes == 2 * HD - 1
            if stage < 2:
                state = jnp.where(last_lane, FAR, 0.0)
            else:
                one_state, other = state_ref[0, pl.ds(row, rows), :], state_ref[1, pl.ds(row, rows), :]
                tops = one_state[:, 2 * HD - 1 :], other[:, 2 * HD - 1 :]
                top = jnp.maximum(*tops)
                state = one_state * jnp.exp2(tops[0] - top) + other * jnp.exp2(tops[1] - top)
                state = jnp.where(last_lane, top, state)
            q = jnp.concatenate([q_ref[:, pl.ds(column, HD)], onehot], axis=1)
            for key, count in tiles:
                s = scores(q, key, count)
                old = state[:, 2 * HD - 1 :]
                top = jnp.maximum(old, jnp.max(s, axis=1, keepdims=True))
                weights = jnp.exp2(s - top).astype(bf16)
                update = product(weights, vx[key : key + count, :], ((1,), (0,)))
                state = state * jnp.exp2(old - top) + update
                state = jnp.where(last_lane, top, state)
            if stage < 2:
                state_ref[0, pl.ds(row, rows), :] = state
            else:
                out_ref[:, pl.ds(column, HD)] = divided(state)
            return carry

        lax.fori_loop(0, heads, one, 0)
        for i in range(PARTS):
            copy_out(i).start()
        for i in range(PARTS):
            copy_out(i).wait()


def attend(stage, back, ring, doc_lengths, guard, queries, kvs, states):
    rows, width = queries.shape
    keys = sum(kv.shape[0] for kv in kvs)
    heads = width // HD
    smem = pl.BlockSpec(memory_space=pltpu.SMEM)
    vmem = pl.BlockSpec(memory_space=pltpu.VMEM)
    hbm = pl.BlockSpec(memory_space=pltpu.HBM)
    guards = [guard] if stage else []
    args = [doc_lengths] + guards + [queries] + kvs + states
    in_specs = [smem] * (1 + len(guards)) + [vmem] * (1 + len(kvs)) + [hbm] * len(states)
    if stage < 2:
        out_shape = [jax.ShapeDtypeStruct((heads * rows, 2 * HD), f32), jax.ShapeDtypeStruct((2,), f32)]
        out_specs = [hbm, smem]
    else:
        out_shape = jax.ShapeDtypeStruct(queries.shape, bf16)
        out_specs = hbm
    return pl.pallas_call(
        partial(kernel, stage, back, ring),
        out_shape=out_shape,
        in_specs=in_specs,
        out_specs=out_specs,
        scratch_shapes=[
            pltpu.VMEM((1 if stage < 2 else 2, heads * rows, 2 * HD), f32),
            pltpu.VMEM((8, HD) if stage < 2 else (heads * rows // PARTS, 2 * HD), f32),
            pltpu.VMEM((16, HD) if stage < 2 else (rows, width), bf16),
            pltpu.VMEM((keys, 2 * HD), bf16),
            pltpu.VMEM((keys, 2 * HD), bf16),
            pltpu.SemaphoreType.DMA((PARTS + 2,)),
        ],
        compiler_params=pltpu.CompilerParams(vmem_limit_bytes=VMEM_BYTES[stage]),
        cost_estimate=pl.CostEstimate(
            flops=8 * heads * rows * keys * HD,
            bytes_accessed=2 * rows * width + heads * rows * HD * 8,
            transcendentals=heads * rows * keys,
        ),
    )(*args)


def passed_along(x, by):
    count = lax.axis_size("qctx")
    return lax.ppermute(x, "qctx", [(i, i + by) for i in range(count - by)])


def to_parts(upward, downward):
    fine = lax.axis_size("kctx")
    later = jnp.arange(fine)[:, None, None] > lax.axis_index("kctx")
    return jnp.where(later, upward[None], downward[None])


def beside(keys, values):
    low = jnp.array(-jnp.inf, bf16)
    keys = lax.pad(keys, low, ((0, 0, 0), (0, HD, 0)))
    return jnp.maximum(keys, lax.pad(values, low, ((0, 0, 0), (HD, 0, 0))))


def shards(queries, keys, values, doc_lengths):
    ring = lax.axis_size("kctx") * queries.shape[0]
    flat = lambda x: x.reshape(-1, 2 * HD)
    own = beside(keys, values)
    one_back = passed_along(own, 1)
    near_parts, held = lax.optimization_barrier((to_parts(own, one_back), one_back))
    near = lax.all_to_all(near_parts, "kctx", 0, 0)
    two_back = passed_along(held, 1)
    far_parts = to_parts(held[:CUT], two_back[:CUT])
    own_state, guard = attend(0, (), ring, doc_lengths, None, queries, [own], [])
    far_parts, guard = lax.optimization_barrier((far_parts, guard))
    far = lax.all_to_all(far_parts, "kctx", 0, 0)
    rest = passed_along(near[:, CUT:], 1)
    near_state, guard = attend(1, ((0, 0),), ring, doc_lengths, guard, queries, [flat(near)], [])
    far_rings = ((1, 0), (1, CUT))
    return attend(
        2, far_rings, ring, doc_lengths, guard, queries, [flat(far), flat(rest)], [own_state, near_state]
    )


def solution(mesh):
    placed = P(("qctx", "kctx"), "head")
    return jax.shard_map(
        shards, mesh=mesh, in_specs=(placed, placed, placed, P()), out_specs=placed, check_vma=False
    )
```

```python
from functools import partial

import jax
import jax.numpy as jnp
from jax import lax
from jax.experimental import pallas as pl
from jax.experimental.pallas import tpu as pltpu
from jax.sharding import PartitionSpec as P

HD = 128
SUB = 2
LEAN_TILE = 512
VMEM_BYTES = 50 * 2**20
PARTS = 2
TILE = 512
SCALE = HD**-0.5 * 1.4426950408889634
SAFE = 100.0
FAR = -(2.0**100)

bf16 = jnp.bfloat16
f32 = jnp.float32


def product(a, b, dims):
    return lax.dot_general(a, b, (dims, ((), ())), preferred_element_type=f32)


def largest_norm(x):
    squares = (x.astype(f32) * x.astype(f32)).astype(bf16)
    sums = product(squares, jnp.ones((HD, HD), bf16), ((1,), (0,)))
    return jnp.max(sums) * 1.02


def kernel(first, back, *refs):
    if first:
        lengths, q_ref, kv_ref, own_ref, out_hbm, guard_out, *scratch = refs
    else:
        lengths, guard_in, q_ref, kv_ref, state_hbm, out_hbm, *scratch = refs
    state_ref, held_ref, out_ref, apart, sems = scratch
    keys = kv_ref.shape[0]
    rows, width = q_ref.shape
    heads = width // HD
    size = SUB * rows
    block, part = lax.axis_index("qctx"), lax.axis_index("kctx")

    def copy_out(i):
        if first:
            here = pl.ds(i * (heads // PARTS) * rows, heads // PARTS * rows)
            return pltpu.make_async_copy(state_ref.at[here], out_hbm.at[here], sems.at[i])
        here = pl.ds(i * (width // PARTS), width // PARTS)
        return pltpu.make_async_copy(out_ref.at[:, here], out_hbm.at[:, here], sems.at[i])

    if not first:
        get_state = pltpu.make_async_copy(state_hbm, state_ref, sems.at[PARTS])
        get_state.start()

    lane = lax.broadcasted_iota(jnp.int32, (1, HD), 1)
    starts = jnp.zeros((1, HD), jnp.int32)
    ends = jnp.zeros((1, HD), jnp.int32)
    run = jnp.int32(0)
    for d in range(lengths.shape[0]):
        starts = jnp.where(lane == d, run, starts)
        run = run + lengths[d]
        ends = jnp.where(lane == d, run, ends)
    slots = keys // rows
    at = lax.broadcasted_iota(jnp.int32, (rows, HD), 0)
    query_start = block * keys + part * rows
    mine = (at >= starts - query_start) & (at < ends - query_start)
    onehot = jnp.where(mine, 1.0, 0.0).astype(bf16)
    for j in range(slots):
        base = (block - back) * keys + j * rows - jnp.where(j >= part, keys, 0)
        inside = (at >= starts - base) & (at < ends - base)
        apart[j * rows : (j + 1) * rows, :] = jnp.where(inside, 0.0, FAR).astype(bf16)
    if first:
        apart[keys:, :] = jnp.where(mine, 0.0, FAR).astype(bf16)

    def kv_rows(key, count):
        return own_ref[...] if key == keys else kv_ref[key : key + count, :]

    def wide_keys(key, count):
        return jnp.concatenate([kv_rows(key, count)[:, 0:HD], apart[key : key + count, :]], axis=1)

    def wide_values(key, count):
        return jnp.concatenate([kv_rows(key, count)[:, HD:], jnp.ones((count, HD), bf16)], axis=1)

    knorm = largest_norm(kv_ref[:, 0:HD])
    if first:
        knorm = jnp.maximum(knorm, largest_norm(own_ref[:, 0:HD]))
        qnorm = largest_norm(q_ref[:, 0:HD])
        for h in range(1, heads):
            qnorm = jnp.maximum(qnorm, largest_norm(q_ref[:, h * HD : (h + 1) * HD]))
    else:
        qnorm = guard_in[1]
    plain = qnorm * knorm <= (SAFE / SCALE) ** 2
    if first:
        guard_out[0] = plain.astype(f32)
        guard_out[1] = qnorm
    else:
        plain = plain & (guard_in[0] == 1.0)

    def scores(q, key, count):
        s = product(q, wide_keys(key, count), ((1,), (1,))) * SCALE
        if key == keys:
            r = lax.broadcasted_iota(jnp.int32, (rows, rows), 0)
            c = lax.broadcasted_iota(jnp.int32, (rows, rows), 1)
            s = jnp.where(jnp.concatenate([c <= r] * (q.shape[0] // rows), axis=0), s, FAR)
        return s

    def tiles(tile):
        return [(key, tile) for key in range(0, keys, tile)] + ([(keys, rows)] if first else [])

    def divided(part):
        total = jnp.broadcast_to(part[:, HD : HD + 1], (rows, HD))
        return (part[:, 0:HD] / total).astype(bf16)

    def update_of(head):
        q = [jnp.concatenate([q_ref[:, h * HD : (h + 1) * HD], onehot], axis=1) for h in range(head, head + SUB)]
        q = jnp.concatenate(q, axis=0)
        total = None
        for key, count in tiles(TILE):
            weights = jnp.exp2(scores(q, key, count)).astype(bf16)
            update = product(weights, wide_values(key, count), ((1,), (0,)))
            total = update if total is None else total + update
        return total

    def finish(head, state):
        for n in range(SUB):
            column = (head + n) * HD
            out_ref[:, column : column + HD] = divided(state[n * rows : (n + 1) * rows])

    for i in range(PARTS):
        group = range(i * heads // PARTS, (i + 1) * heads // PARTS, SUB)
        for head in group:
            here = slice(head * rows, head * rows + size)
            if first:
                state = update_of(head)
                lanes = lax.broadcasted_iota(jnp.int32, state.shape, 1)
                state_ref[here, :] = jnp.where(lanes == 2 * HD - 1, 0.0, state)
            elif i == 0:
                held_ref[here, :] = update_of(head)
            else:
                finish(head, state_ref[here, :] + update_of(head))
        if not first and i == 0:
            get_state.wait()
            for head in group:
                here = slice(head * rows, head * rows + size)
                finish(head, state_ref[here, :] + held_ref[here, :])
        copy_out(i).start()
    for i in range(PARTS):
        copy_out(i).wait()

    @pl.when(jnp.logical_not(plain))
    def _():
        def one(head, carry):
            row = pl.multiple_of(head * rows, rows)
            column = pl.multiple_of(head * HD, HD)
            lanes = lax.broadcasted_iota(jnp.int32, (rows, 2 * HD), 1)
            if first:
                state = jnp.where(lanes == 2 * HD - 1, FAR, 0.0)
            else:
                state = state_ref[pl.ds(row, rows), :]
            q = jnp.concatenate([q_ref[:, pl.ds(column, HD)], onehot], axis=1)
            for key, count in reversed(tiles(LEAN_TILE)):
                s = scores(q, key, count)
                old = state[:, 2 * HD - 1 :]
                top = jnp.maximum(old, jnp.max(s, axis=1, keepdims=True))
                weights = jnp.exp2(s - top).astype(bf16)
                update = product(weights, wide_values(key, count), ((1,), (0,)))
                state = state * jnp.exp2(old - top) + update
                state = jnp.where(lanes == 2 * HD - 1, top, state)
            if first:
                state_ref[pl.ds(row, rows), :] = state
            else:
                out_ref[:, pl.ds(column, HD)] = divided(state)
            return carry

        lax.fori_loop(0, heads, one, 0)
        for i in range(PARTS):
            copy_out(i).start()
        for i in range(PARTS):
            copy_out(i).wait()


def attend(first, back, doc_lengths, queries, kv, *rest):
    rows, width = queries.shape
    keys = kv.shape[0]
    every = keys + rows if first else keys
    heads = width // HD
    smem = pl.BlockSpec(memory_space=pltpu.SMEM)
    vmem = pl.BlockSpec(memory_space=pltpu.VMEM)
    hbm = pl.BlockSpec(memory_space=pltpu.HBM)
    if first:
        args = (doc_lengths, queries, kv) + rest
        in_specs = [smem, vmem, vmem, vmem]
        out_shape = [jax.ShapeDtypeStruct((heads * rows, 2 * HD), f32), jax.ShapeDtypeStruct((2,), f32)]
        out_specs = [hbm, smem]
    else:
        state, guard = rest
        args = (doc_lengths, guard, queries, kv, state)
        in_specs = [smem, smem, vmem, vmem, hbm]
        out_shape = jax.ShapeDtypeStruct(queries.shape, bf16)
        out_specs = hbm
    return pl.pallas_call(
        partial(kernel, first, back),
        out_shape=out_shape,
        in_specs=in_specs,
        out_specs=out_specs,
        scratch_shapes=[
            pltpu.VMEM((heads * rows, 2 * HD), f32),
            pltpu.VMEM((8, HD) if first else (heads * rows // PARTS, 2 * HD), f32),
            pltpu.VMEM((8, HD) if first else (rows, width), bf16),
            pltpu.VMEM((every, HD), bf16),
            pltpu.SemaphoreType.DMA((PARTS + 1,)),
        ],
        compiler_params=pltpu.CompilerParams(vmem_limit_bytes=VMEM_BYTES),
        cost_estimate=pl.CostEstimate(
            flops=8 * heads * rows * every * HD,
            bytes_accessed=2 * rows * width + heads * rows * HD * 8,
            transcendentals=heads * rows * every,
        ),
    )(*args)


def passed_along(x, by):
    count = lax.axis_size("qctx")
    return lax.ppermute(x, "qctx", [(i, i + by) for i in range(count - by)])


def to_parts(upward, downward):
    fine = lax.axis_size("kctx")
    later = jnp.arange(fine)[:, None, None] > lax.axis_index("kctx")
    return jnp.where(later, upward[None], downward[None])


def beside(keys, values):
    low = jnp.array(-jnp.inf, bf16)
    keys = lax.pad(keys, low, ((0, 0, 0), (0, HD, 0)))
    return jnp.maximum(keys, lax.pad(values, low, ((0, 0, 0), (HD, 0, 0))))


def shards(queries, keys, values, doc_lengths):
    block_rows = lax.axis_size("kctx") * queries.shape[0]
    own = beside(keys, values)
    one_back = passed_along(own, 1)
    near_parts, held = lax.optimization_barrier((to_parts(own, one_back), one_back))
    near = lax.all_to_all(near_parts, "kctx", 0, 0).reshape(block_rows, 2 * HD)
    two_back = passed_along(held, 1)
    far = lax.all_to_all(to_parts(held, two_back), "kctx", 0, 0).reshape(block_rows, 2 * HD)
    carried = attend(True, 0, doc_lengths, queries, near, own)
    return attend(False, 1, doc_lengths, queries, far, *carried)


def solution(mesh):
    placed = P(("qctx", "kctx"), "head")
    return jax.shard_map(
        shards, mesh=mesh, in_specs=(placed, placed, placed, P()), out_specs=placed, check_vma=False
    )
```

```python
from functools import partial

import jax
import jax.numpy as jnp
from jax import lax
from jax.experimental import pallas as pl
from jax.experimental.pallas import tpu as pltpu
from jax.sharding import PartitionSpec as P

HD = 128
SUB = 4
LEAN_TILE = 512
VMEM_BYTES = 50 * 2**20
PARTS = 2
TILES = {True: 256, False: 1536}
SCALE = HD**-0.5 * 1.4426950408889634
SAFE = 100.0
FAR = -(2.0**100)

bf16 = jnp.bfloat16
f32 = jnp.float32


def product(a, b, dims):
    return lax.dot_general(a, b, (dims, ((), ())), preferred_element_type=f32)


def largest_norm(x):
    squares = (x.astype(f32) * x.astype(f32)).astype(bf16)
    sums = product(squares, jnp.ones((HD, HD), bf16), ((1,), (0,)))
    return jnp.max(sums) * 1.02


def kernel(first, back, *refs):
    if first:
        lengths, q_ref, kv_ref, own_ref, out_hbm, guard_out, *scratch = refs
    else:
        lengths, guard_in, q_ref, kv_ref, state_hbm, out_hbm, *scratch = refs
    state_ref, held_ref, out_ref, apart, sems = scratch
    keys = kv_ref.shape[0]
    rows, width = q_ref.shape
    heads = width // HD
    size = SUB * rows
    block, part = lax.axis_index("qctx"), lax.axis_index("kctx")

    def copy_out(i):
        if first:
            here = pl.ds(i * (heads // PARTS) * rows, heads // PARTS * rows)
            return pltpu.make_async_copy(state_ref.at[here], out_hbm.at[here], sems.at[i])
        here = pl.ds(i * (width // PARTS), width // PARTS)
        return pltpu.make_async_copy(out_ref.at[:, here], out_hbm.at[:, here], sems.at[i])

    if not first:
        get_state = pltpu.make_async_copy(state_hbm, state_ref, sems.at[PARTS])
        get_state.start()

    lane = lax.broadcasted_iota(jnp.int32, (1, HD), 1)
    starts = jnp.zeros((1, HD), jnp.int32)
    ends = jnp.zeros((1, HD), jnp.int32)
    run = jnp.int32(0)
    for d in range(lengths.shape[0]):
        starts = jnp.where(lane == d, run, starts)
        run = run + lengths[d]
        ends = jnp.where(lane == d, run, ends)
    slots = keys // rows
    at = lax.broadcasted_iota(jnp.int32, (rows, HD), 0)
    query_start = block * keys + part * rows
    mine = (at >= starts - query_start) & (at < ends - query_start)
    onehot = jnp.where(mine, 1.0, 0.0).astype(bf16)
    for j in range(slots):
        base = (block - back) * keys + j * rows - jnp.where(j >= part, keys, 0)
        inside = (at >= starts - base) & (at < ends - base)
        apart[j * rows : (j + 1) * rows, :] = jnp.where(inside, 0.0, FAR).astype(bf16)
    if first:
        apart[keys:, :] = jnp.where(mine, 0.0, FAR).astype(bf16)

    def kv_rows(key, count):
        return own_ref[...] if key == keys else kv_ref[key : key + count, :]

    def wide_keys(key, count):
        return jnp.concatenate([kv_rows(key, count)[:, 0:HD], apart[key : key + count, :]], axis=1)

    def wide_values(key, count):
        return jnp.concatenate([kv_rows(key, count)[:, HD:], jnp.ones((count, HD), bf16)], axis=1)

    knorm = largest_norm(kv_ref[:, 0:HD])
    if first:
        knorm = jnp.maximum(knorm, largest_norm(own_ref[:, 0:HD]))
        qnorm = largest_norm(q_ref[:, 0:HD])
        for h in range(1, heads):
            qnorm = jnp.maximum(qnorm, largest_norm(q_ref[:, h * HD : (h + 1) * HD]))
    else:
        qnorm = guard_in[1]
    plain = qnorm * knorm <= (SAFE / SCALE) ** 2
    if first:
        guard_out[0] = plain.astype(f32)
        guard_out[1] = qnorm
    else:
        plain = plain & (guard_in[0] == 1.0)

    def scores(q, key, count):
        s = product(q, wide_keys(key, count), ((1,), (1,))) * SCALE
        if key == keys:
            r = lax.broadcasted_iota(jnp.int32, (rows, rows), 0)
            c = lax.broadcasted_iota(jnp.int32, (rows, rows), 1)
            s = jnp.where(jnp.concatenate([c <= r] * (q.shape[0] // rows), axis=0), s, FAR)
        return s

    def tiles(tile):
        return [(key, tile) for key in range(0, keys, tile)] + ([(keys, rows)] if first else [])

    def divided(part):
        total = jnp.broadcast_to(part[:, HD : HD + 1], (rows, HD))
        return (part[:, 0:HD] / total).astype(bf16)

    def update_of(head):
        q = [jnp.concatenate([q_ref[:, h * HD : (h + 1) * HD], onehot], axis=1) for h in range(head, head + SUB)]
        q = jnp.concatenate(q, axis=0)
        total = None
        for key, count in tiles(TILES[first]):
            weights = jnp.exp2(scores(q, key, count)).astype(bf16)
            update = product(weights, wide_values(key, count), ((1,), (0,)))
            total = update if total is None else total + update
        return total

    def finish(head, state):
        for n in range(SUB):
            column = (head + n) * HD
            out_ref[:, column : column + HD] = divided(state[n * rows : (n + 1) * rows])

    for i in range(PARTS):
        group = range(i * heads // PARTS, (i + 1) * heads // PARTS, SUB)
        for head in group:
            here = slice(head * rows, head * rows + size)
            if first:
                state = update_of(head)
                lanes = lax.broadcasted_iota(jnp.int32, state.shape, 1)
                state_ref[here, :] = jnp.where(lanes == 2 * HD - 1, 0.0, state)
            elif i == 0:
                held_ref[here, :] = update_of(head)
            else:
                finish(head, state_ref[here, :] + update_of(head))
        if not first and i == 0:
            get_state.wait()
            for head in group:
                here = slice(head * rows, head * rows + size)
                finish(head, state_ref[here, :] + held_ref[here, :])
        copy_out(i).start()
    for i in range(PARTS):
        copy_out(i).wait()

    @pl.when(jnp.logical_not(plain))
    def _():
        def one(head, carry):
            row = pl.multiple_of(head * rows, rows)
            column = pl.multiple_of(head * HD, HD)
            lanes = lax.broadcasted_iota(jnp.int32, (rows, 2 * HD), 1)
            if first:
                state = jnp.where(lanes == 2 * HD - 1, FAR, 0.0)
            else:
                state = state_ref[pl.ds(row, rows), :]
            q = jnp.concatenate([q_ref[:, pl.ds(column, HD)], onehot], axis=1)
            for key, count in reversed(tiles(LEAN_TILE)):
                s = scores(q, key, count)
                old = state[:, 2 * HD - 1 :]
                top = jnp.maximum(old, jnp.max(s, axis=1, keepdims=True))
                weights = jnp.exp2(s - top).astype(bf16)
                update = product(weights, wide_values(key, count), ((1,), (0,)))
                state = state * jnp.exp2(old - top) + update
                state = jnp.where(lanes == 2 * HD - 1, top, state)
            if first:
                state_ref[pl.ds(row, rows), :] = state
            else:
                out_ref[:, pl.ds(column, HD)] = divided(state)
            return carry

        lax.fori_loop(0, heads, one, 0)
        for i in range(PARTS):
            copy_out(i).start()
        for i in range(PARTS):
            copy_out(i).wait()


def attend(first, back, doc_lengths, queries, kv, *rest):
    rows, width = queries.shape
    keys = kv.shape[0]
    every = keys + rows if first else keys
    heads = width // HD
    smem = pl.BlockSpec(memory_space=pltpu.SMEM)
    vmem = pl.BlockSpec(memory_space=pltpu.VMEM)
    hbm = pl.BlockSpec(memory_space=pltpu.HBM)
    if first:
        args = (doc_lengths, queries, kv) + rest
        in_specs = [smem, vmem, vmem, vmem]
        out_shape = [jax.ShapeDtypeStruct((heads * rows, 2 * HD), f32), jax.ShapeDtypeStruct((2,), f32)]
        out_specs = [hbm, smem]
    else:
        state, guard = rest
        args = (doc_lengths, guard, queries, kv, state)
        in_specs = [smem, smem, vmem, vmem, hbm]
        out_shape = jax.ShapeDtypeStruct(queries.shape, bf16)
        out_specs = hbm
    return pl.pallas_call(
        partial(kernel, first, back),
        out_shape=out_shape,
        in_specs=in_specs,
        out_specs=out_specs,
        scratch_shapes=[
            pltpu.VMEM((heads * rows, 2 * HD), f32),
            pltpu.VMEM((8, HD) if first else (heads * rows // PARTS, 2 * HD), f32),
            pltpu.VMEM((8, HD) if first else (rows, width), bf16),
            pltpu.VMEM((every, HD), bf16),
            pltpu.SemaphoreType.DMA((PARTS + 1,)),
        ],
        compiler_params=pltpu.CompilerParams(vmem_limit_bytes=VMEM_BYTES),
        cost_estimate=pl.CostEstimate(
            flops=8 * heads * rows * every * HD,
            bytes_accessed=2 * rows * width + heads * rows * HD * 8,
            transcendentals=heads * rows * every,
        ),
    )(*args)


def passed_along(x, by):
    count = lax.axis_size("qctx")
    return lax.ppermute(x, "qctx", [(i, i + by) for i in range(count - by)])


def to_parts(upward, downward):
    fine = lax.axis_size("kctx")
    later = jnp.arange(fine)[:, None, None] > lax.axis_index("kctx")
    return jnp.where(later, upward[None], downward[None])


def beside(keys, values):
    low = jnp.array(-jnp.inf, bf16)
    keys = lax.pad(keys, low, ((0, 0, 0), (0, HD, 0)))
    return jnp.maximum(keys, lax.pad(values, low, ((0, 0, 0), (HD, 0, 0))))


def shards(queries, keys, values, doc_lengths):
    block_rows = lax.axis_size("kctx") * queries.shape[0]
    own = beside(keys, values)
    one_back = passed_along(own, 1)
    near_parts, held = lax.optimization_barrier((to_parts(own, one_back), one_back))
    near = lax.all_to_all(near_parts, "kctx", 0, 0).reshape(block_rows, 2 * HD)
    two_back = passed_along(held, 1)
    far = lax.all_to_all(to_parts(held, two_back), "kctx", 0, 0).reshape(block_rows, 2 * HD)
    carried = attend(True, 0, doc_lengths, queries, near, own)
    return attend(False, 1, doc_lengths, queries, far, *carried)


def solution(mesh):
    placed = P(("qctx", "kctx"), "head")
    return jax.shard_map(
        shards, mesh=mesh, in_specs=(placed, placed, placed, P()), out_specs=placed, check_vma=False
    )
```
